32 devices in a mesh: atom: 8 (over z, core), wave: 4 (over y, x).
Axes of the slice: x: 2, y: 2, z: 4, core: 2. Of those that a mesh axis runs over, the one named last changes fastest.
Arguments:
- features: bfloat16 [16384, 128], P(('atom', 'wave')), may hold values from -6 to 6
- species: int32 [16384], P(('atom', 'wave')), may hold values from 0 to 15
- coords: float32 [3, 16384], P(None, ('atom', 'wave')), may hold values from 0 to 1
- wave_index: int32 [3, 4096], P(None, 'wave'), may hold values from -16 to 16, as said below
- green: float32 [4096], P('wave'), may hold values from 4.8828126e-05 to 0.00048828125
- embed: bfloat16 [16, 128], replicated, may hold values from -3 to 3
- w_charge: bfloat16 [128, 64], replicated, may hold values from -0.5 to 0.5
- w_feat: bfloat16 [128, 256], replicated, may hold values from -0.5 to 0.5
- w_pot: bfloat16 [64, 256], replicated, may hold values from -0.75 to 0.75
- w_out: bfloat16 [256, 128], replicated, may hold values from -0.375 to 0.375
Outputs:
- updated: bfloat16 [16384, 128], P(('atom', 'wave'))
The draws below stay inside these ranges and needn't reach their ends.
Inputs may be any that keep to these rules, and one draw needn't show every extreme that they name: `wave_index`: the 4096 wave vectors are distinct lattice vectors, and none is zero.
All inputs are finite; a program needn't handle non-finite values.
Results may differ from the reference program's by a relative error of at most 0.0075.
Values may be sent and summed in bfloat16 or wider, within the bound.
No kernel may reach another device: no remote copies, remote signals or barrier semaphores. Data moves between devices by JAX's collectives and lax.ppermute only.
A program may use at most 128 MiB of HBM per device.

```python
import math
import jax
import jax.numpy as jnp
from jax import lax

F = 128
Q = 64
HID = 256
SPECIES = 16
NATOMS = 16384
KWAVES = 4096


def draw_wave_index(key, part):
    order = jax.random.permutation(jax.random.fold_in(key, 71), 35936)
    points = order[:KWAVES].astype(jnp.int32)
    points = points + (points >= 17968).astype(jnp.int32)
    first = points // 1089 - 16
    second = points // 33 % 33 - 16
    third = points % 33 - 16
    return jnp.stack([first, second, third]).astype(jnp.int32)


def touch_ends(result, key, smallest, top_value):
    shape = result.shape
    spot = [jax.random.randint(jax.random.fold_in(key, axis), (), 0, shape[axis]) for axis in range(len(shape))]
    result = result.at[tuple(spot)].set(smallest)
    longest = shape.index(max(shape))
    spot[longest] = (spot[longest] + 1) % shape[longest]
    return result.at[tuple(spot)].set(top_value)


def shard_levels(rng, dims, cuts, least, largest):
    factor_of = 1.0
    for position, blocks in cuts:
        heights = jax.random.uniform(jax.random.fold_in(jax.random.fold_in(rng, 6), position), (blocks,), jnp.float32, least / len(cuts), largest / len(cuts))
        factor_of = factor_of * jnp.repeat(jnp.exp(heights), dims[position] // blocks).reshape((-1,) + (1,) * (len(dims) - 1 - position))
    return factor_of


def normal_values(stream_key, shape, spread, bound, cuts=(), kind=jnp.bfloat16):
    result = jax.random.normal(stream_key, shape, jnp.float32) * spread
    if len(cuts) > 0:
        result = shard_levels(stream_key, shape, cuts, -0.22, 0.18) * result
    return jnp.clip(result, min=-bound, max=bound).astype(kind)


def setup_inputs(seed: int = 0) -> dict:
    key_of = jax.random.split(jax.random.key(seed), 11)
    return {
        "features": normal_values(key_of[0], (NATOMS, F), 1.0, 6.0, ((0, 32),)),
        "species": touch_ends(jax.random.randint(key_of[1], (NATOMS,), 0, SPECIES), jax.random.fold_in(key_of[1], 1), 0, SPECIES - 1).astype(jnp.int32),
        "coords": jnp.clip(1.0 * jax.random.uniform(key_of[2], (3, NATOMS), jnp.float32) ** shard_levels(key_of[2], (3, NATOMS), ((1, 32),), -0.2, 0.2), 0.0, 1.0),
        "wave_index": draw_wave_index(jax.random.fold_in(key_of[10], 71), 0),
        "green": jnp.clip(jnp.exp(math.log(0.00048828125) - 2.3025851 * jax.random.uniform(key_of[4], (KWAVES,), jnp.float32) ** shard_levels(key_of[4], (KWAVES,), ((0, 4),), -0.2, 0.2)), 4.882812572759576e-05, 0.00048828125),
        "embed": normal_values(key_of[5], (SPECIES, F), 0.5, 3.0),
        "w_charge": normal_values(key_of[6], (F, Q), F ** -0.5, 0.5),
        "w_feat": normal_values(key_of[7], (F, HID), F ** -0.5, 0.5),
        "w_pot": normal_values(key_of[8], (Q, HID), Q ** -0.5, 0.75),
        "w_out": normal_values(key_of[9], (HID, F), HID ** -0.5, 0.375),
    }


TWO_PI = 2.0 * math.pi
EPS = 1e-06

def phases(points, waves):
    angle = points[0][:, None] * waves[0][None, :] + points[1][:, None] * waves[1][None, :]
    angle = TWO_PI * (angle + points[2][:, None] * waves[2][None, :])
    return jnp.concatenate([jnp.cos(angle), jnp.sin(angle)], axis=1).astype(jnp.bfloat16)

def reference(features, species, coords, wave_index, green, embed, w_charge, w_feat, w_pot, w_out):
    hidden_in = features.astype(jnp.float32)
    scale = lax.rsqrt(lax.optimization_barrier(jnp.mean(hidden_in * hidden_in, axis=1, keepdims=True)) + EPS)
    onehot = (species[:, None] == jnp.arange(SPECIES, dtype=jnp.int32)[None, :]).astype(jnp.bfloat16)
    mixed = hidden_in * scale + jnp.dot(onehot, embed, preferred_element_type=jnp.float32)
    mixed_b = mixed.astype(jnp.bfloat16)
    charges = jnp.dot(mixed_b, w_charge, preferred_element_type=jnp.float32).astype(jnp.bfloat16)
    waves = wave_index.astype(jnp.float32)
    step = math.gcd(NATOMS, 2048)
    count = NATOMS // step
    point_blocks = coords.reshape(3, count, step).transpose(1, 0, 2)
    charge_blocks = charges.reshape(count, step, Q)

    def add_block(total, item):
        points, block_charges = item
        tile = phases(points, waves)
        part = lax.dot_general(tile, block_charges, (((0,), (0,)), ((), ())), preferred_element_type=jnp.float32)
        return (total + part, None)
    start = jnp.zeros((2 * KWAVES, Q), jnp.float32)
    structure, _ = lax.scan(add_block, start, (point_blocks, charge_blocks))
    green_both = jnp.concatenate([green, green])
    weighted = (green_both[:, None] * structure).astype(jnp.bfloat16)

    def potential_block(points):
        return jnp.dot(phases(points, waves), weighted, preferred_element_type=jnp.float32)
    potential = lax.map(potential_block, point_blocks).reshape(NATOMS, Q)
    potential_b = potential.astype(jnp.bfloat16)
    pre = jnp.dot(mixed_b, w_feat, preferred_element_type=jnp.float32) + jnp.dot(potential_b, w_pot, preferred_element_type=jnp.float32)
    activation = jax.nn.silu(pre).astype(jnp.bfloat16)
    return (hidden_in + jnp.dot(activation, w_out, preferred_element_type=jnp.float32)).astype(jnp.bfloat16)
```

```python
import functools
import math

import jax
import jax.numpy as jnp
import numpy as np
from jax import lax
from jax.experimental import pallas as pl
from jax.experimental.pallas import tpu as pltpu
from jax.sharding import PartitionSpec as P

EPS = 1e-06
F32 = jnp.float32
BF16 = jnp.bfloat16
VMEM = pl.BlockSpec(memory_space=pltpu.VMEM)
POINT_ROWS = 16
CORES = 2


def fit(values, degree, count=4000):
    u = (np.cos(np.pi * (np.arange(count) + 0.5) / count) + 1) / 8
    cheb = np.polynomial.chebyshev.Chebyshev.fit(u, values(np.sqrt(u)), degree, domain=[0, 0.25])
    return [float(c) for c in cheb.convert(kind=np.polynomial.Polynomial).coef]


HALF_SIN = fit(lambda r: math.sqrt(2) * np.sin(np.pi * r) / r, 3)
HALF_COS = fit(lambda r: math.sqrt(2) * np.cos(np.pi * r), 3)


def horner(coefs, u):
    total = coefs[-1]
    for c in coefs[-2::-1]:
        total = total * u + c
    return total


def phase_rows(n, x):
    turns = jnp.dot(n, x, preferred_element_type=F32)
    r = turns - jnp.round(turns)
    u = r * r
    s = horner(HALF_SIN, u) * r
    c = horner(HALF_COS, u)
    return jnp.concatenate([1.0 - s * s, s * c], axis=0).astype(BF16)


def nt(a, b):
    return lax.dot_general(a, b, (((1,), (1,)), ((), ())), preferred_element_type=F32)


def tn(a, b):
    return lax.dot_general(a, b, (((0,), (0,)), ((), ())), preferred_element_type=F32)


def triple_rows(values, width):
    row = lax.broadcasted_iota(jnp.int32, (POINT_ROWS, width), 0)
    part = row % 3
    picked = jnp.where(part == 0, values[0:1], jnp.where(part == 1, values[1:2], values[2:3]))
    return row, picked


def pre_kernel(features_ref, species_ref, coords_ref, embed_ref, w_charge_ref, mixed_ref, message_ref):
    rows = features_ref.shape[0]
    q = w_charge_ref.shape[1]
    hidden = features_ref[...].astype(F32)
    scale = lax.rsqrt(jnp.mean(hidden * hidden, axis=1, keepdims=True) + EPS)
    kinds = embed_ref.shape[0]
    onehot = (
        lax.broadcasted_iota(jnp.int32, (kinds, rows), 0) == species_ref[...]
    ).astype(F32).astype(BF16)
    mixed = (hidden * scale + tn(onehot, embed_ref[...])).astype(BF16)
    mixed_ref[...] = mixed
    charges = lax.dot_general(
        w_charge_ref[...], mixed, (((0,), (1,)), ((), ())), preferred_element_type=F32
    )
    message_ref[0:q, :] = charges.astype(BF16)
    row, point = triple_rows(coords_ref[...], rows)
    high = point.astype(BF16).astype(F32)
    middle = (point - high).astype(BF16).astype(F32)
    low = point - high - middle
    parts = jnp.where(row < 3, high, jnp.where(row < 6, middle, jnp.where(row < 9, low, 0.0)))
    message_ref[q:, :] = parts.astype(BF16)


def own_kernel(zcount, kchunk, waves_ref, message_ref, n_ref, p_own_ref, p_other_ref, s_own_ref, s_other_ref, all_n):
    width = waves_ref.shape[1]
    q = message_ref.shape[0] - POINT_ROWS
    row, index = triple_rows(waves_ref[...].astype(F32), width)
    all_n[...] = jnp.where(row < 9, index, 0.0).T
    me = lax.axis_index("atom")
    z, core = me // CORES, me % CORES
    x = message_ref[q:, :]
    charges = message_ref[0:q, :]
    for half, (p_ref, s_ref) in enumerate(((p_own_ref, s_own_ref), (p_other_ref, s_other_ref))):
        for r in range(zcount):
            j = (z ^ r) * CORES + (core ^ half)
            n = all_n[pl.ds(pl.multiple_of(j * kchunk, kchunk), kchunk), :].astype(BF16)
            at = (half * zcount + r) * kchunk
            n_ref[at : at + kchunk, :] = n
            rows = phase_rows(n, x)
            lo = r * 2 * kchunk
            p_ref[lo : lo + 2 * kchunk, :] = rows
            s_ref[:, lo : lo + 2 * kchunk] = nt(charges, rows)


def half_kernel(half, zcount, kchunk, rounded, count, *refs):
    n_ref, s_in_ref = refs[0], refs[1]
    messages = refs[2 : 2 + count]
    p_ref, s_ref = refs[2 + count :]
    q = messages[0].shape[0] - POINT_ROWS
    atoms = messages[0].shape[1]
    for r in range(zcount):
        at = (half * zcount + r) * kchunk
        n = n_ref[at : at + kchunk, :]
        lo = r * 2 * kchunk
        total = s_in_ref[:, lo : lo + 2 * kchunk]
        for b, message_ref in enumerate(messages):
            rows = phase_rows(n, message_ref[q:, :])
            p_ref[lo : lo + 2 * kchunk, b * atoms : (b + 1) * atoms] = rows
            total = total + nt(message_ref[0:q, :], rows)
        s_ref[:, lo : lo + 2 * kchunk] = total.astype(s_ref.dtype)


def share_kernel(s_ref, got_ref, mine_ref, *send_refs):
    width = mine_ref.shape[1]
    for r, ref in enumerate((mine_ref,) + send_refs):
        part = s_ref[:, r * width : (r + 1) * width] + got_ref[:, r * width : (r + 1) * width].astype(F32)
        ref[...] = part.astype(ref.dtype)


def weight_kernel(mine_ref, green_ref, *refs):
    out_ref = refs[-1]
    total = mine_ref[...]
    for ref in refs[:-1]:
        total = total + ref[...].astype(F32)
    me = lax.axis_index("atom")
    green = green_ref[pl.ds(me, 1), :]
    out_ref[...] = (total * jnp.concatenate([green, green], axis=1)).astype(BF16)


def first_half_kernel(w_ref, p0_ref, p_ref, own_ref, rest_ref):
    own_ref[...] = jnp.dot(w_ref[...], p0_ref[...], preferred_element_type=F32)
    rest_ref[...] = jnp.dot(w_ref[...], p_ref[...], preferred_element_type=F32)


def send_half_kernel(w_ref, p_ref, rest_ref, *send_refs):
    atoms = send_refs[0].shape[1]
    for b, ref in enumerate(send_refs):
        part = jnp.dot(w_ref[...], p_ref[:, b * atoms : (b + 1) * atoms], preferred_element_type=F32)
        ref[...] = (rest_ref[:, b * atoms : (b + 1) * atoms] + part).astype(BF16)


def keep_half_kernel(w_ref, p0_ref, own_ref, mixed_ref, w_feat_ref, total_ref, pre_ref):
    total_ref[...] = own_ref[...] + jnp.dot(w_ref[...], p0_ref[...], preferred_element_type=F32)
    pre_ref[...] = jnp.dot(mixed_ref[...], w_feat_ref[...], preferred_element_type=F32)


def last_kernel(features_ref, total_ref, pre_ref, w_pot_ref, w_out_ref, *refs):
    out_ref = refs[-1]
    potential = total_ref[...]
    for ref in refs[:-1]:
        potential = potential + ref[...].astype(F32)
    pre = pre_ref[...] + tn(potential.astype(BF16), w_pot_ref[...])
    activation = (pre / (1.0 + jnp.exp(-pre))).astype(BF16)
    out = features_ref[...].astype(F32) + jnp.dot(activation, w_out_ref[...], preferred_element_type=F32)
    out_ref[...] = out.astype(BF16)


def call(kernel, outs, *args, scratch=(), flops=0):
    size = sum(math.prod(a.shape) * a.dtype.itemsize for a in (*args, *outs))
    limit = min(max(4 * size, 16 << 20), 56 << 20)
    return pl.pallas_call(
        kernel,
        out_shape=outs,
        in_specs=[VMEM] * len(args),
        out_specs=[VMEM] * len(outs),
        scratch_shapes=list(scratch),
        compiler_params=pltpu.CompilerParams(vmem_limit_bytes=limit),
        cost_estimate=pl.CostEstimate(flops=flops, bytes_accessed=size, transcendentals=0),
    )(*args)


def swap(value, axis, bit):
    count = lax.axis_size(axis)
    return lax.ppermute(value, axis, [(i, i ^ bit) for i in range(count)])


def shards(features, species, coords, wave_index, green, embed, w_charge, w_feat, w_pot, w_out):
    array = jax.ShapeDtypeStruct
    atoms = features.shape[0]
    q = w_charge.shape[1]
    hidden = w_feat.shape[1]
    waves = wave_index.shape[1]
    wcount = lax.axis_size("wave")
    acount = lax.axis_size("atom")
    zcount = acount // CORES
    kchunk = waves // acount
    half_rows = 2 * kchunk * zcount
    rest = (wcount - 1) * atoms

    mixed, message = call(
        pre_kernel,
        [array(features.shape, BF16), array((q + POINT_ROWS, atoms), BF16)],
        features, species.reshape(1, atoms), coords, embed, w_charge,
    )
    messages = [swap(message, "wave", b) for b in range(1, wcount)]
    n, p_own0, p_other0, s_own0, s_other0 = call(
        functools.partial(own_kernel, zcount, kchunk),
        [
            array((waves, POINT_ROWS), BF16),
            array((half_rows, atoms), BF16),
            array((half_rows, atoms), BF16),
            array((q, half_rows), F32),
            array((q, half_rows), F32),
        ],
        wave_index, message,
        scratch=[pltpu.VMEM((waves, POINT_ROWS), F32)],
        flops=4 * half_rows * atoms * q,
    )

    def half_call(half, s_in, dtype):
        return call(
            functools.partial(half_kernel, half, zcount, kchunk, None, wcount - 1),
            [array((half_rows, rest), BF16), array((q, half_rows), dtype)],
            n, s_in, *messages,
            flops=2 * half_rows * rest * q,
        )

    p_other, s_other = half_call(1, s_other0, BF16)
    got = swap(s_other, "atom", 1)
    p_own, s_own = half_call(0, s_own0, F32)
    chunk = (q, 2 * kchunk)
    mine, *shares = call(
        share_kernel,
        [array(chunk, F32)] + [array(chunk, BF16)] * (zcount - 1),
        s_own, got,
    )
    shares = [swap(value, "atom", CORES * (r + 1)) for r, value in enumerate(shares)]
    (weighted,) = call(
        weight_kernel, [array(chunk, BF16)], mine, green.reshape(acount, kchunk), *shares
    )
    w_own = jnp.concatenate(
        [weighted] + [swap(weighted, "atom", CORES * r) for r in range(1, zcount)], axis=1
    )
    w_other = swap(w_own, "atom", 1)
    own_a, rest_a = call(
        first_half_kernel,
        [array((q, atoms), F32), array((q, rest), F32)],
        w_own, p_own0, p_own,
        flops=2 * half_rows * (rest + atoms) * q,
    )
    sends = call(
        send_half_kernel, [array((q, atoms), BF16)] * (wcount - 1), w_other, p_other, rest_a,
        flops=2 * half_rows * rest * q,
    )
    parts = [swap(value, "wave", b + 1) for b, value in enumerate(sends)]
    total, pre = call(
        keep_half_kernel,
        [array((q, atoms), F32), array((atoms, hidden), F32)],
        w_other, p_other0, own_a, mixed, w_feat,
        flops=2 * half_rows * atoms * q,
    )
    (out,) = call(
        last_kernel, [array(features.shape, BF16)],
        features, total, pre, w_pot, w_out, *parts,
    )
    return out


def solution(mesh):
    placed = (
        P(("atom", "wave"), None),
        P(("atom", "wave")),
        P(None, ("atom", "wave")),
        P(None, "wave"),
        P("wave"),
        P(),
        P(),
        P(),
        P(),
        P(),
    )
    return jax.shard_map(
        shards, mesh=mesh, in_specs=placed, out_specs=P(("atom", "wave"), None), check_vma=False
    )
```

```python
import functools
import math

import jax
import jax.numpy as jnp
import numpy as np
from jax import lax
from jax.experimental import pallas as pl
from jax.experimental.pallas import tpu as pltpu
from jax.sharding import PartitionSpec as P

EPS = 1e-06
F32 = jnp.float32
BF16 = jnp.bfloat16
VMEM = pl.BlockSpec(memory_space=pltpu.VMEM)
POINT_ROWS = 16
CORES = 2
TILE = 128
PIECES = 2


def fit(values, degree, count=4000):
    u = (np.cos(np.pi * (np.arange(count) + 0.5) / count) + 1) / 8
    cheb = np.polynomial.chebyshev.Chebyshev.fit(u, values(np.sqrt(u)), degree, domain=[0, 0.25])
    return [float(c) for c in cheb.convert(kind=np.polynomial.Polynomial).coef]


HALF_SIN = fit(lambda r: math.sqrt(2) * np.sin(np.pi * r) / r, 3)
HALF_COS = fit(lambda r: math.sqrt(2) * np.cos(np.pi * r), 3)


def horner(coefs, u):
    total = coefs[-1]
    for c in coefs[-2::-1]:
        total = total * u + c
    return total


def phase_rows(n, x):
    turns = jnp.dot(n, x, preferred_element_type=F32)
    r = turns - jnp.round(turns)
    u = r * r
    s = horner(HALF_SIN, u) * r
    c = horner(HALF_COS, u)
    return jnp.concatenate([1.0 - s * s, s * c], axis=0).astype(BF16)


def nt(a, b):
    return lax.dot_general(a, b, (((1,), (1,)), ((), ())), preferred_element_type=F32)


def tn(a, b):
    return lax.dot_general(a, b, (((0,), (0,)), ((), ())), preferred_element_type=F32)


def triple_rows(values, width):
    row = lax.broadcasted_iota(jnp.int32, (POINT_ROWS, width), 0)
    part = row % 3
    picked = jnp.where(part == 0, values[0:1], jnp.where(part == 1, values[1:2], values[2:3]))
    return row, picked


def fetch_kernel(
    features_ref, species_ref, coords_ref, waves_ref, green_ref, embed_ref, w_charge_ref,
    hidden_ref, mixed_ref, message_ref, waves_out, green_out,
    species_v, coords_v, embed_v, w_charge_v, sems,
):
    pairs = (
        (features_ref, hidden_ref), (embed_ref, embed_v), (species_ref, species_v),
        (w_charge_ref, w_charge_v), (coords_ref, coords_v), (waves_ref, waves_out), (green_ref, green_out),
    )
    copies = [pltpu.make_async_copy(a, b, sems.at[i]) for i, (a, b) in enumerate(pairs)]
    for copy in copies:
        copy.start()
    for copy in copies:
        copy.wait()
    rows = hidden_ref.shape[0]
    q = w_charge_v.shape[0]
    hidden = hidden_ref[...].astype(F32)
    scale = lax.rsqrt(jnp.mean(hidden * hidden, axis=1, keepdims=True) + EPS)
    kinds = embed_v.shape[0]
    onehot = (
        lax.broadcasted_iota(jnp.int32, (kinds, rows), 0) == species_v[...]
    ).astype(F32).astype(BF16)
    mixed = (hidden * scale + tn(onehot, embed_v[...])).astype(BF16)
    mixed_ref[...] = mixed
    message_ref[0:q, :] = nt(w_charge_v[...], mixed).astype(BF16)
    row, point = triple_rows(coords_v[...], rows)
    high = point.astype(BF16).astype(F32)
    middle = (point - high).astype(BF16).astype(F32)
    low = point - high - middle
    parts = jnp.where(row < 3, high, jnp.where(row < 6, middle, jnp.where(row < 9, low, 0.0)))
    message_ref[q:, :] = parts.astype(BF16)


def own_kernel(
    waves_ref, green_ref, message_ref,
    n_ref, g_ref, p_own_ref, p_other_ref, s_own_ref, s_other_ref,
):
    width = waves_ref.shape[1]
    half = width // CORES
    q = message_ref.shape[0] - POINT_ROWS
    core = lax.axis_index("atom") % CORES
    row, index = triple_rows(waves_ref[...].astype(F32), width)
    index = jnp.where(row < 9, index, 0.0)
    first, second = index[:, :half], index[:, half:]
    n_ref[0:half, :] = jnp.where(core == 0, first, second).T.astype(BF16)
    n_ref[half:, :] = jnp.where(core == 0, second, first).T.astype(BF16)
    green = jnp.where(core == 0, green_ref[:, :half], green_ref[:, half:])
    tile = min(TILE, half)
    for c in range(half // tile):
        g = green[:, c * tile : (c + 1) * tile]
        g_ref[:, 2 * c * tile : 2 * (c + 1) * tile] = jnp.concatenate([g, g], axis=1)
    x = message_ref[q:, :]
    charges = message_ref[0:q, :]
    for h, (p_ref, s_ref) in enumerate(((p_own_ref, s_own_ref), (p_other_ref, s_other_ref))):
        for c in range(half // tile):
            n = n_ref[h * half + c * tile : h * half + (c + 1) * tile, :]
            rows = phase_rows(n, x)
            p_ref[2 * c * tile : 2 * (c + 1) * tile, :] = rows
            s_ref[:, 2 * c * tile : 2 * (c + 1) * tile] = nt(charges, rows)


def rest_kernel(start, span, s_start, count, *refs):
    n_ref, s_in_ref = refs[0], refs[1]
    messages = refs[2 : 2 + count]
    p_ref, s_ref = refs[2 + count :]
    q = messages[0].shape[0] - POINT_ROWS
    atoms = messages[0].shape[1]
    tile = min(TILE, span)
    for c in range(span // tile):
        n = n_ref[start + c * tile : start + (c + 1) * tile, :]
        lo, hi = 2 * c * tile, 2 * (c + 1) * tile
        total = s_in_ref[:, s_start + lo : s_start + hi]
        for b, message_ref in enumerate(messages):
            rows = phase_rows(n, message_ref[q:, :])
            p_ref[lo:hi, b * atoms : (b + 1) * atoms] = rows
            total = total + nt(message_ref[0:q, :], rows)
        s_ref[:, lo:hi] = total.astype(s_ref.dtype)


def join_kernel(offset, mine_ref, got_ref, sum_ref, send_ref):
    width = mine_ref.shape[1]
    total = mine_ref[...] + got_ref[:, offset : offset + width].astype(F32)
    sum_ref[...] = total
    send_ref[...] = total.astype(BF16)


def weight_kernel(count, *refs):
    g_ref, out_ref = refs[0], refs[-1]
    at = 0
    for i in range(count):
        mine_ref, got_ref = refs[1 + 2 * i : 3 + 2 * i]
        width = mine_ref.shape[1]
        total = mine_ref[...] + got_ref[...].astype(F32)
        out_ref[:, at : at + width] = (total * g_ref[:, at : at + width]).astype(BF16)
        at += width


def first_half_kernel(pieces, w_ref, p0_ref, *refs):
    own_ref, rest_ref = refs[pieces:]
    own_ref[...] = jnp.dot(w_ref[...], p0_ref[...], preferred_element_type=F32)
    at, total = 0, None
    for p_ref in refs[:pieces]:
        height = p_ref.shape[0]
        part = jnp.dot(w_ref[:, at : at + height], p_ref[...], preferred_element_type=F32)
        total = part if total is None else total + part
        at += height
    rest_ref[...] = total


def send_half_kernel(w_ref, p_ref, rest_ref, *send_refs):
    atoms = send_refs[0].shape[1]
    for b, ref in enumerate(send_refs):
        part = jnp.dot(w_ref[...], p_ref[:, b * atoms : (b + 1) * atoms], preferred_element_type=F32)
        ref[...] = (rest_ref[:, b * atoms : (b + 1) * atoms] + part).astype(BF16)


def keep_half_kernel(w_ref, p0_ref, own_ref, mixed_ref, w_feat_ref, total_ref, pre_ref):
    total_ref[...] = own_ref[...] + jnp.dot(w_ref[...], p0_ref[...], preferred_element_type=F32)
    pre_ref[...] = jnp.dot(mixed_ref[...], w_feat_ref[...], preferred_element_type=F32)


def last_kernel(features_ref, total_ref, pre_ref, w_pot_ref, w_out_ref, *refs):
    out_ref = refs[-1]
    potential = total_ref[...]
    for ref in refs[:-1]:
        potential = potential + ref[...].astype(F32)
    pre = pre_ref[...] + tn(potential.astype(BF16), w_pot_ref[...])
    activation = (pre / (1.0 + jnp.exp(-pre))).astype(BF16)
    out = features_ref[...].astype(F32) + jnp.dot(activation, w_out_ref[...], preferred_element_type=F32)
    out_ref[...] = out.astype(BF16)


def call(kernel, outs, *args, scratch=(), flops=0, space=pltpu.VMEM):
    size = sum(math.prod(a.shape) * a.dtype.itemsize for a in (*args, *outs))
    limit = min(max(4 * size, 16 << 20), 56 << 20)
    if space == pltpu.HBM:
        args = [pltpu.with_memory_space_constraint(a, pltpu.HBM) for a in args]
    return pl.pallas_call(
        kernel,
        out_shape=outs,
        in_specs=[pl.BlockSpec(memory_space=space)] * len(args),
        out_specs=[VMEM] * len(outs),
        scratch_shapes=list(scratch),
        compiler_params=pltpu.CompilerParams(vmem_limit_bytes=limit),
        cost_estimate=pl.CostEstimate(flops=flops, bytes_accessed=size, transcendentals=0),
    )(*args)


def swap(value, axis, bit):
    count = lax.axis_size(axis)
    return lax.ppermute(value, axis, [(i, i ^ bit) for i in range(count)])


def shards(features, species, coords, wave_index, green, embed, w_charge, w_feat, w_pot, w_out):
    array = jax.ShapeDtypeStruct
    atoms = features.shape[0]
    q = w_charge.shape[1]
    hidden = w_feat.shape[1]
    waves = wave_index.shape[1]
    wcount = lax.axis_size("wave")
    acount = lax.axis_size("atom")
    zcount = acount // CORES
    half_rows = 2 * (waves // CORES)
    rest = (wcount - 1) * atoms

    half = waves // CORES
    tile = min(TILE, half)
    pieces = PIECES if (half // tile) % PIECES == 0 else 1
    span = half // pieces

    hidden_v, mixed, message, waves_v, green_v = call(
        fetch_kernel,
        [
            array(features.shape, BF16), array(features.shape, BF16), array((q + POINT_ROWS, atoms), BF16),
            array(wave_index.shape, jnp.int32), array((1, waves), F32),
        ],
        features, species.reshape(1, atoms), coords, wave_index, green.reshape(1, waves), embed, w_charge.T,
        scratch=[
            pltpu.VMEM((1, atoms), jnp.int32), pltpu.VMEM(coords.shape, F32),
            pltpu.VMEM(embed.shape, BF16), pltpu.VMEM((q, features.shape[1]), BF16),
            pltpu.SemaphoreType.DMA((7,)),
        ],
        space=pltpu.HBM,
    )
    messages = [swap(message, "wave", b) for b in range(1, wcount)]
    n, g, p_own0, p_other0, s_own0, s_other0 = call(
        own_kernel,
        [
            array((waves, POINT_ROWS), BF16),
            array((1, half_rows), F32),
            array((half_rows, atoms), BF16),
            array((half_rows, atoms), BF16),
            array((q, half_rows), F32),
            array((q, half_rows), F32),
        ],
        waves_v, green_v, message,
        flops=4 * half_rows * atoms * q,
    )

    def rest_call(start, size, s_start, n, s_in, dtype):
        return call(
            functools.partial(rest_kernel, start, size, s_start, wcount - 1),
            [array((2 * size, rest), BF16), array((q, 2 * size), dtype)],
            n, s_in, *messages,
            flops=4 * size * rest * q,
        )

    def join(mine, got, offset=0):
        shape = mine.shape
        return call(functools.partial(join_kernel, offset), [array(shape, F32), array(shape, BF16)], mine, got)

    p_other, s_other = rest_call(half, half, 0, n, s_other0, BF16)
    got = swap(s_other, "atom", 1)
    p_own, sums, arrived = [], [], []
    for i in range(pieces):
        p, s = rest_call(i * span, span, 2 * i * span, n, s_own0, F32)
        total, send = join(s, got, 2 * i * span)
        p_own.append(p)
        sums.append(total)
        arrived.append(swap(send, "atom", CORES))
        n, sums[-1] = lax.optimization_barrier((n, sums[-1]))
    bit = 2
    while bit < zcount:
        for i in range(pieces):
            sums[i], send = join(sums[i], arrived[i])
            arrived[i] = swap(send, "atom", CORES * bit)
        bit *= 2
    (w_own,) = call(
        functools.partial(weight_kernel, pieces), [array((q, half_rows), BF16)],
        g, *[value for pair in zip(sums, arrived) for value in pair],
    )
    w_other = swap(w_own, "atom", 1)
    own_a, rest_a = call(
        functools.partial(first_half_kernel, pieces),
        [array((q, atoms), F32), array((q, rest), F32)],
        w_own, p_own0, *p_own,
        flops=2 * half_rows * (rest + atoms) * q,
    )
    sends = call(
        send_half_kernel, [array((q, atoms), BF16)] * (wcount - 1), w_other, p_other, rest_a,
        flops=2 * half_rows * rest * q,
    )
    parts = [swap(value, "wave", b + 1) for b, value in enumerate(sends)]
    total, pre = call(
        keep_half_kernel,
        [array((q, atoms), F32), array((atoms, hidden), F32)],
        w_other, p_other0, own_a, mixed, w_feat,
        flops=2 * half_rows * atoms * q,
    )
    (out,) = call(
        last_kernel, [array(features.shape, BF16)],
        hidden_v, total, pre, w_pot, w_out, *parts,
    )
    return out


def solution(mesh):
    placed = (
        P(("atom", "wave"), None),
        P(("atom", "wave")),
        P(None, ("atom", "wave")),
        P(None, "wave"),
        P("wave"),
        P(),
        P(),
        P(),
        P(),
        P(),
    )
    return jax.shard_map(
        shards, mesh=mesh, in_specs=placed, out_specs=P(("atom", "wave"), None), check_vma=False
    )
```

```python
import functools
import math

import jax
import jax.numpy as jnp
import numpy as np
from jax import lax
from jax.experimental import pallas as pl
from jax.experimental.pallas import tpu as pltpu
from jax.sharding import PartitionSpec as P

EPS = 1e-06
F32 = jnp.float32
BF16 = jnp.bfloat16
POINT_ROWS = 16
CORES = 2
TILE = 128
MARGIN = 2e-6
PIECES = 2
OUT_PARTS = 4


def half_sine():
    u = (np.cos(np.pi * np.arange(4) / 3) + 1) / 8
    r = np.sqrt(np.maximum(u, 1e-16))
    return [float(c) for c in np.polynomial.polynomial.polyfit(u, math.sqrt(2) * np.sin(np.pi * r) / r, 3)]


HALF_SINE = half_sine()


def phases(turns):
    r = turns - jnp.round(turns)
    u = r * r
    total = HALF_SINE[-1]
    for c in HALF_SINE[-2::-1]:
        total = total * u + c
    s = total * r
    q = s * s
    rest = (2.0 + MARGIN) - q
    return (1.0 - q).astype(BF16), (s * (rest * lax.rsqrt(rest))).astype(BF16)


def put_phases(p_ref, lo, tile, left, n, x):
    cosine, sine = phases(jnp.dot(n, x, preferred_element_type=F32))
    right = left + x.shape[1]
    p_ref[lo : lo + tile, left:right] = cosine
    p_ref[lo + tile : lo + 2 * tile, left:right] = sine


def nt(a, b):
    return lax.dot_general(a, b, (((1,), (1,)), ((), ())), preferred_element_type=F32)


def tn(a, b):
    return lax.dot_general(a, b, (((0,), (0,)), ((), ())), preferred_element_type=F32)


def triple_rows(values, width):
    row = lax.broadcasted_iota(jnp.int32, (POINT_ROWS, width), 0)
    part = row % 3
    picked = jnp.where(part == 0, values[0:1], jnp.where(part == 1, values[1:2], values[2:3]))
    return row, picked


def fetch_kernel(
    features_ref, species_ref, coords_ref, waves_ref, green_ref, embed_ref, w_charge_ref,
    hidden_ref, mixed_ref, message_ref, waves_out, green_out,
    species_v, coords_v, embed_v, w_charge_v, sems,
):
    pairs = (
        (features_ref, hidden_ref), (embed_ref, embed_v), (species_ref, species_v),
        (w_charge_ref, w_charge_v), (coords_ref, coords_v), (waves_ref, waves_out), (green_ref, green_out),
    )
    copies = [pltpu.make_async_copy(a, b, sems.at[i]) for i, (a, b) in enumerate(pairs)]
    for copy in copies:
        copy.start()
    for copy in copies:
        copy.wait()
    rows = hidden_ref.shape[0]
    q = w_charge_v.shape[0]
    hidden = hidden_ref[...].astype(F32)
    scale = lax.rsqrt(jnp.mean(hidden * hidden, axis=1, keepdims=True) + EPS)
    kinds = embed_v.shape[0]
    onehot = (
        lax.broadcasted_iota(jnp.int32, (kinds, rows), 0) == species_v[...]
    ).astype(F32).astype(BF16)
    mixed = (hidden * scale + tn(onehot, embed_v[...])).astype(BF16)
    mixed_ref[...] = mixed
    message_ref[0:q, :] = nt(w_charge_v[...], mixed).astype(BF16)
    row, point = triple_rows(coords_v[...], rows)
    high = point.astype(BF16).astype(F32)
    middle = (point - high).astype(BF16).astype(F32)
    low = point - high - middle
    parts = jnp.where(row < 3, high, jnp.where(row < 6, middle, jnp.where(row < 9, low, 0.0)))
    message_ref[q:, :] = parts.astype(BF16)


def own_kernel(
    pieces, waves_ref, green_ref, message_ref,
    n_ref, g_ref, p_own_ref, p_other_ref, s_own_ref, s_other_ref,
):
    width = waves_ref.shape[1]
    half = width // CORES
    span = half // pieces
    tile = min(TILE, span)
    q = message_ref.shape[0] - POINT_ROWS
    core = lax.axis_index("atom") % CORES
    row, index = triple_rows(waves_ref[...].astype(F32), width)
    index = jnp.where(row < 9, index, 0.0)

    def pick(values, h, i):
        at = i * span
        first, second = values[:, at : at + span], values[:, half + at : half + at + span]
        return jnp.where(core == h, first, second)

    for h in range(CORES):
        for i in range(pieces):
            at = h * half + i * span
            n_ref[at : at + span, :] = pick(index, h, i).T.astype(BF16)
    for i in range(pieces):
        green = pick(green_ref[...], 0, i)
        for c in range(span // tile):
            g = green[:, c * tile : (c + 1) * tile]
            lo = 2 * (i * span + c * tile)
            g_ref[:, lo : lo + 2 * tile] = jnp.concatenate([g, g], axis=1)
    x = message_ref[q:, :]
    for h, (p_ref, s_ref) in enumerate(((p_own_ref, s_own_ref), (p_other_ref, s_other_ref))):
        for c in range(half // tile):
            lo = 2 * c * tile
            put_phases(p_ref, lo, tile, 0, n_ref[h * half + c * tile : h * half + (c + 1) * tile, :], x)
            s_ref[:, lo : lo + 2 * tile] = nt(message_ref[0:q, :], p_ref[lo : lo + 2 * tile, :])


def rest_kernel(start, span, tile, s_start, count, *refs):
    n_ref, s_in_ref = refs[0], refs[1]
    messages = refs[2 : 2 + count]
    p_ref, s_ref, charges = refs[2 + count :]
    q = messages[0].shape[0] - POINT_ROWS
    atoms = messages[0].shape[1]
    for b, message_ref in enumerate(messages):
        charges[:, b * atoms : (b + 1) * atoms] = message_ref[0:q, :]
    for c in range(span // tile):
        n = n_ref[start + c * tile : start + (c + 1) * tile, :]
        lo, hi = 2 * c * tile, 2 * (c + 1) * tile
        for b, message_ref in enumerate(messages):
            put_phases(p_ref, lo, tile, b * atoms, n, message_ref[q:, :])
        total = s_in_ref[:, s_start + lo : s_start + hi] + nt(charges[...], p_ref[lo:hi, :])
        s_ref[:, lo:hi] = total.astype(s_ref.dtype)


def join_kernel(offset, count, *refs):
    outs = refs[1 + count :]
    width = refs[0].shape[1]
    total = refs[0][...]
    for i, ref in enumerate(refs[1 : 1 + count]):
        at = offset if i == 0 else 0
        total = total + ref[:, at : at + width].astype(F32)
    for ref in outs:
        ref[...] = total.astype(ref.dtype)


def weight_kernel(count, *refs):
    g_ref, out_ref = refs[0], refs[-1]
    at = 0
    for i in range(count):
        mine_ref, got_ref = refs[1 + 2 * i : 3 + 2 * i]
        width = mine_ref.shape[1]
        total = mine_ref[...] + got_ref[...].astype(F32)
        out_ref[:, at : at + width] = (total * g_ref[:, at : at + width]).astype(BF16)
        at += width


def potential_kernel(pieces, w_ref, p0_ref, *refs):
    own_ref, rest_ref = refs[pieces:]
    own_ref[...] = jnp.dot(w_ref[...], p0_ref[...], preferred_element_type=F32)
    at, total = 0, None
    for p_ref in refs[:pieces]:
        height = p_ref.shape[0]
        part = jnp.dot(w_ref[:, at : at + height], p_ref[...], preferred_element_type=F32)
        total = part if total is None else total + part
        at += height
    rest_ref[...] = total


def send_kernel(w_ref, p_ref, rest_ref, *send_refs):
    atoms = send_refs[0].shape[1]
    for b, ref in enumerate(send_refs):
        part = jnp.dot(w_ref[...], p_ref[:, b * atoms : (b + 1) * atoms], preferred_element_type=F32)
        ref[...] = (rest_ref[:, b * atoms : (b + 1) * atoms] + part).astype(BF16)


def keep_kernel(w_ref, p0_ref, own_ref, mixed_ref, w_feat_ref, total_ref, pre_ref):
    total_ref[...] = own_ref[...] + jnp.dot(w_ref[...], p0_ref[...], preferred_element_type=F32)
    pre_ref[...] = jnp.dot(mixed_ref[...], w_feat_ref[...], preferred_element_type=F32)


def last_kernel(count, hidden_ref, total_ref, pre_ref, w_pot_ref, w_out_ref, *refs):
    out_ref, out_v, sems = refs[count:]
    atoms = hidden_ref.shape[0]
    step = atoms // OUT_PARTS
    copies = []
    for i in range(OUT_PARTS):
        at = i * step
        potential = total_ref[:, at : at + step]
        for ref in refs[:count]:
            potential = potential + ref[:, at : at + step].astype(F32)
        pre = pre_ref[at : at + step, :] + tn(potential.astype(BF16), w_pot_ref[...])
        activation = (0.5 * pre * (1.0 + jnp.tanh(0.5 * pre))).astype(BF16)
        out = hidden_ref[at : at + step, :].astype(F32) + jnp.dot(
            activation, w_out_ref[...], preferred_element_type=F32
        )
        out_v[at : at + step, :] = out.astype(BF16)
        copy = pltpu.make_async_copy(out_v.at[at : at + step, :], out_ref.at[at : at + step, :], sems.at[i])
        copy.start()
        copies.append(copy)
    for copy in copies:
        copy.wait()


def call(kernel, outs, *args, scratch=(), flops=0, space=pltpu.VMEM, out_space=pltpu.VMEM):
    size = sum(math.prod(a.shape) * a.dtype.itemsize for a in (*args, *outs))
    limit = min(max(4 * size, 16 << 20), 56 << 20)
    if space == pltpu.HBM:
        args = [pltpu.with_memory_space_constraint(a, pltpu.HBM) for a in args]
    return pl.pallas_call(
        kernel,
        out_shape=outs,
        in_specs=[pl.BlockSpec(memory_space=space)] * len(args),
        out_specs=[pl.BlockSpec(memory_space=out_space)] * len(outs),
        scratch_shapes=list(scratch),
        compiler_params=pltpu.CompilerParams(vmem_limit_bytes=limit),
        cost_estimate=pl.CostEstimate(flops=flops, bytes_accessed=size, transcendentals=0),
    )(*args)


def swap(value, axis, bit):
    count = lax.axis_size(axis)
    return lax.ppermute(value, axis, [(i, i ^ bit) for i in range(count)])


def z_swap(value, step):
    count = lax.axis_size("atom")
    steps = (count // CORES).bit_length() - 1
    bits = [CORES << s for s in range(steps)]
    return lax.ppermute(
        value, "atom", [(i, i ^ bits[step if i % CORES == 0 else steps - 1 - step]) for i in range(count)]
    )


def shards(features, species, coords, wave_index, green, embed, w_charge, w_feat, w_pot, w_out):
    array = jax.ShapeDtypeStruct
    atoms = features.shape[0]
    q = w_charge.shape[1]
    hidden = w_feat.shape[1]
    waves = wave_index.shape[1]
    wcount = lax.axis_size("wave")
    acount = lax.axis_size("atom")
    zcount = acount // CORES
    half_rows = 2 * (waves // CORES)
    rest = (wcount - 1) * atoms

    half = waves // CORES
    pieces = PIECES if (half // min(TILE, half)) % PIECES == 0 else 1
    span = half // pieces
    tile = min(TILE, span)

    hidden_v, mixed, message, waves_v, green_v = call(
        fetch_kernel,
        [
            array(features.shape, BF16), array(features.shape, BF16), array((q + POINT_ROWS, atoms), BF16),
            array(wave_index.shape, jnp.int32), array((1, waves), F32),
        ],
        features, species.reshape(1, atoms), coords, wave_index, green.reshape(1, waves), embed, w_charge.T,
        scratch=[
            pltpu.VMEM((1, atoms), jnp.int32), pltpu.VMEM(coords.shape, F32),
            pltpu.VMEM(embed.shape, BF16), pltpu.VMEM((q, features.shape[1]), BF16),
            pltpu.SemaphoreType.DMA((7,)),
        ],
        space=pltpu.HBM,
    )
    messages = [swap(message, "wave", b) for b in range(1, wcount)]
    n, g, p_own0, p_other0, s_own0, s_other0 = call(
        functools.partial(own_kernel, pieces),
        [
            array((waves, POINT_ROWS), BF16),
            array((1, half_rows), F32),
            array((half_rows, atoms), BF16),
            array((half_rows, atoms), BF16),
            array((q, half_rows), F32),
            array((q, half_rows), F32),
        ],
        waves_v, green_v, message,
        flops=4 * half_rows * atoms * q,
    )

    def rest_call(start, size, s_start, n, s_in, dtype):
        return call(
            functools.partial(rest_kernel, start, size, tile, s_start, wcount - 1),
            [array((2 * size, rest), BF16), array((q, 2 * size), dtype)],
            n, s_in, *messages,
            scratch=[pltpu.VMEM((q, rest), BF16)],
            flops=4 * size * rest * q,
        )

    def join(outs, mine, *got, offset=0):
        return call(
            functools.partial(join_kernel, offset, len(got)), [array(mine.shape, dtype) for dtype in outs], mine, *got
        )

    rows = 2 * span
    p_other, s_other = rest_call(half, half, 0, n, s_other0, BF16)
    got = swap(s_other, "atom", 1)
    p_own, sums, arrived = [], [], []
    for i in range(pieces):
        p, total = rest_call(i * span, span, i * rows, n, s_own0, F32)
        p_own.append(p)
        total, send = join([F32, BF16], total, got, offset=i * rows)
        sums.append(total)
        arrived.append(z_swap(send, 0))
        n, sums[-1] = lax.optimization_barrier((n, sums[-1]))
    for step in range(1, zcount.bit_length() - 1):
        for i in range(pieces):
            sums[i], send = join([F32, BF16], sums[i], arrived[i])
            arrived[i] = z_swap(send, step)
    (w_own,) = call(
        functools.partial(weight_kernel, pieces), [array((q, half_rows), BF16)],
        g, *[value for pair in zip(sums, arrived) for value in pair],
    )
    w_other = swap(w_own, "atom", 1)
    own, others = call(
        functools.partial(potential_kernel, pieces), [array((q, atoms), F32), array((q, rest), F32)],
        w_own, p_own0, *p_own,
        flops=2 * half_rows * (rest + atoms) * q,
    )
    sends = call(
        send_kernel, [array((q, atoms), BF16)] * (wcount - 1), w_other, p_other, others,
        flops=2 * half_rows * rest * q,
    )
    order = sorted(range(wcount - 1), key=lambda b: -bin(b + 1).count("1"))
    parts = [swap(sends[b], "wave", b + 1) for b in order]
    total, pre = call(
        keep_kernel,
        [array((q, atoms), F32), array((atoms, hidden), F32)],
        w_other, p_other0, own, mixed, w_feat,
        flops=2 * half_rows * atoms * q,
    )
    (out,) = call(
        functools.partial(last_kernel, wcount - 1), [array(features.shape, BF16)],
        hidden_v, total, pre, w_pot, w_out, *parts,
        scratch=[pltpu.VMEM(features.shape, BF16), pltpu.SemaphoreType.DMA((OUT_PARTS,))],
        out_space=pl.ANY,
    )
    return out


def solution(mesh):
    placed = (
        P(("atom", "wave"), None),
        P(("atom", "wave")),
        P(None, ("atom", "wave")),
        P(None, "wave"),
        P("wave"),
        P(),
        P(),
        P(),
        P(),
        P(),
    )
    return jax.shard_map(
        shards, mesh=mesh, in_specs=placed, out_specs=P(("atom", "wave"), None), check_vma=False
    )
```

```python
import functools
import math

import jax
import jax.numpy as jnp
import numpy as np
from jax import lax
from jax.experimental import pallas as pl
from jax.experimental.pallas import tpu as pltpu
from jax.sharding import PartitionSpec as P

EPS = 1e-06
F32 = jnp.float32
BF16 = jnp.bfloat16
POINT_ROWS = 16
CORES = 2
TILE = 128
MARGIN = 2e-6
PIECES = 2
OUT_PARTS = 4


def half_sine():
    u = (np.cos(np.pi * np.arange(4) / 3) + 1) / 8
    r = np.sqrt(np.maximum(u, 1e-16))
    return [float(c) for c in np.polynomial.polynomial.polyfit(u, math.sqrt(2) * np.sin(np.pi * r) / r, 3)]


HALF_SINE = half_sine()


def phases(turns):
    r = turns - jnp.round(turns)
    u = r * r
    total = HALF_SINE[-1]
    for c in HALF_SINE[-2::-1]:
        total = total * u + c
    s = total * r
    q = s * s
    rest = (2.0 + MARGIN) - q
    return (1.0 - q).astype(BF16), (s * (rest * lax.rsqrt(rest))).astype(BF16)


def put_phases(p_ref, lo, tile, left, n, x):
    cosine, sine = phases(jnp.dot(n, x, preferred_element_type=F32))
    right = left + x.shape[1]
    p_ref[lo : lo + tile, left:right] = cosine
    p_ref[lo + tile : lo + 2 * tile, left:right] = sine


def nt(a, b):
    return lax.dot_general(a, b, (((1,), (1,)), ((), ())), preferred_element_type=F32)


def tn(a, b):
    return lax.dot_general(a, b, (((0,), (0,)), ((), ())), preferred_element_type=F32)


def triple_rows(values, width):
    row = lax.broadcasted_iota(jnp.int32, (POINT_ROWS, width), 0)
    part = row % 3
    picked = jnp.where(part == 0, values[0:1], jnp.where(part == 1, values[1:2], values[2:3]))
    return row, picked


def fetch_kernel(
    features_ref, species_ref, coords_ref, waves_ref, green_ref, embed_ref, w_charge_ref,
    hidden_ref, mixed_ref, message_ref, waves_out, green_out,
    species_v, coords_v, embed_v, w_charge_v, sems,
):
    pairs = (
        (features_ref, hidden_ref), (embed_ref, embed_v), (species_ref, species_v),
        (w_charge_ref, w_charge_v), (coords_ref, coords_v), (waves_ref, waves_out), (green_ref, green_out),
    )
    copies = [pltpu.make_async_copy(a, b, sems.at[i]) for i, (a, b) in enumerate(pairs)]
    for copy in copies:
        copy.start()
    for copy in copies:
        copy.wait()
    rows = hidden_ref.shape[0]
    q = w_charge_v.shape[0]
    hidden = hidden_ref[...].astype(F32)
    scale = lax.rsqrt(jnp.mean(hidden * hidden, axis=1, keepdims=True) + EPS)
    kinds = embed_v.shape[0]
    onehot = (
        lax.broadcasted_iota(jnp.int32, (kinds, rows), 0) == species_v[...]
    ).astype(F32).astype(BF16)
    mixed = (hidden * scale + tn(onehot, embed_v[...])).astype(BF16)
    mixed_ref[...] = mixed
    message_ref[0:q, :] = nt(w_charge_v[...], mixed).astype(BF16)
    row, point = triple_rows(coords_v[...], rows)
    high = point.astype(BF16).astype(F32)
    middle = (point - high).astype(BF16).astype(F32)
    low = point - high - middle
    parts = jnp.where(row < 3, high, jnp.where(row < 6, middle, jnp.where(row < 9, low, 0.0)))
    message_ref[q:, :] = parts.astype(BF16)


def own_kernel(
    pieces, waves_ref, green_ref, message_ref,
    n_ref, g_ref, p_own_ref, p_other_ref, s_own_ref, s_other_ref,
):
    width = waves_ref.shape[1]
    half = width // CORES
    span = half // pieces
    tile = min(TILE, span)
    q = message_ref.shape[0] - POINT_ROWS
    core = lax.axis_index("atom") % CORES
    row, index = triple_rows(waves_ref[...].astype(F32), width)
    index = jnp.where(row < 9, index, 0.0)

    def pick(values, h, i):
        at = i * span
        first, second = values[:, at : at + span], values[:, half + at : half + at + span]
        return jnp.where(core == h, first, second)

    for h in range(CORES):
        for i in range(pieces):
            at = h * half + i * span
            n_ref[at : at + span, :] = pick(index, h, i).T.astype(BF16)
    for i in range(pieces):
        green = pick(green_ref[...], 0, i)
        for c in range(span // tile):
            g = green[:, c * tile : (c + 1) * tile]
            lo = 2 * (i * span + c * tile)
            g_ref[:, lo : lo + 2 * tile] = jnp.concatenate([g, g], axis=1)
    x = message_ref[q:, :]
    for h, (p_ref, s_ref) in enumerate(((p_own_ref, s_own_ref), (p_other_ref, s_other_ref))):
        for c in range(half // tile):
            lo = 2 * c * tile
            put_phases(p_ref, lo, tile, 0, n_ref[h * half + c * tile : h * half + (c + 1) * tile, :], x)
            s_ref[:, lo : lo + 2 * tile] = nt(message_ref[0:q, :], p_ref[lo : lo + 2 * tile, :])


def rest_kernel(start, span, tile, s_start, count, *refs):
    n_ref, s_in_ref = refs[0], refs[1]
    messages = refs[2 : 2 + count]
    p_ref, s_ref, charges = refs[2 + count :]
    q = messages[0].shape[0] - POINT_ROWS
    atoms = messages[0].shape[1]
    for b, message_ref in enumerate(messages):
        charges[:, b * atoms : (b + 1) * atoms] = message_ref[0:q, :]
    for c in range(span // tile):
        n = n_ref[start + c * tile : start + (c + 1) * tile, :]
        lo, hi = 2 * c * tile, 2 * (c + 1) * tile
        for b, message_ref in enumerate(messages):
            put_phases(p_ref, lo, tile, b * atoms, n, message_ref[q:, :])
        total = s_in_ref[:, s_start + lo : s_start + hi] + nt(charges[...], p_ref[lo:hi, :])
        s_ref[:, lo:hi] = total.astype(s_ref.dtype)


def join_kernel(offset, count, *refs):
    outs = refs[1 + count :]
    width = refs[0].shape[1]
    total = refs[0][...]
    for i, ref in enumerate(refs[1 : 1 + count]):
        at = offset if i == 0 else 0
        total = total + ref[:, at : at + width].astype(F32)
    for ref in outs:
        ref[...] = total.astype(ref.dtype)


def weight_kernel(count, *refs):
    g_ref, out_ref = refs[0], refs[-1]
    at = 0
    for i in range(count):
        mine_ref, got_ref = refs[1 + 2 * i : 3 + 2 * i]
        width = mine_ref.shape[1]
        total = mine_ref[...] + got_ref[...].astype(F32)
        out_ref[:, at : at + width] = (total * g_ref[:, at : at + width]).astype(BF16)
        at += width


def potential_kernel(pieces, w_ref, p0_ref, *refs):
    own_ref, rest_ref = refs[pieces:]
    own_ref[...] = jnp.dot(w_ref[...], p0_ref[...], preferred_element_type=F32)
    at, total = 0, None
    for p_ref in refs[:pieces]:
        height = p_ref.shape[0]
        part = jnp.dot(w_ref[:, at : at + height], p_ref[...], preferred_element_type=F32)
        total = part if total is None else total + part
        at += height
    rest_ref[...] = total


def send_kernel(w_ref, p_ref, rest_ref, *send_refs):
    atoms = send_refs[0].shape[1]
    core = lax.axis_index("atom") % CORES
    for b, ref in enumerate(send_refs):
        block = jnp.where(core == 0, len(send_refs) - 1 - b, b)
        here = pl.ds(pl.multiple_of(block * atoms, atoms), atoms)
        part = jnp.dot(w_ref[...], p_ref[:, here], preferred_element_type=F32)
        ref[...] = (rest_ref[:, here] + part).astype(BF16)


def keep_kernel(w_ref, p0_ref, own_ref, mixed_ref, w_feat_ref, total_ref, pre_ref):
    total_ref[...] = own_ref[...] + jnp.dot(w_ref[...], p0_ref[...], preferred_element_type=F32)
    pre_ref[...] = jnp.dot(mixed_ref[...], w_feat_ref[...], preferred_element_type=F32)


def last_kernel(count, hidden_ref, total_ref, pre_ref, w_pot_ref, w_out_ref, *refs):
    out_ref, out_v, sems = refs[count:]
    atoms = hidden_ref.shape[0]
    step = atoms // OUT_PARTS
    copies = []
    for i in range(OUT_PARTS):
        at = i * step
        potential = total_ref[:, at : at + step]
        for ref in refs[:count]:
            potential = potential + ref[:, at : at + step].astype(F32)
        pre = pre_ref[at : at + step, :] + tn(potential.astype(BF16), w_pot_ref[...])
        activation = (0.5 * pre * (1.0 + jnp.tanh(0.5 * pre))).astype(BF16)
        out = hidden_ref[at : at + step, :].astype(F32) + jnp.dot(
            activation, w_out_ref[...], preferred_element_type=F32
        )
        out_v[at : at + step, :] = out.astype(BF16)
        copy = pltpu.make_async_copy(out_v.at[at : at + step, :], out_ref.at[at : at + step, :], sems.at[i])
        copy.start()
        copies.append(copy)
    for copy in copies:
        copy.wait()


def call(kernel, outs, *args, scratch=(), flops=0, space=pltpu.VMEM, out_space=pltpu.VMEM):
    size = sum(math.prod(a.shape) * a.dtype.itemsize for a in (*args, *outs))
    limit = min(max(4 * size, 16 << 20), 56 << 20)
    if space == pltpu.HBM:
        args = [pltpu.with_memory_space_constraint(a, pltpu.HBM) for a in args]
    return pl.pallas_call(
        kernel,
        out_shape=outs,
        in_specs=[pl.BlockSpec(memory_space=space)] * len(args),
        out_specs=[pl.BlockSpec(memory_space=out_space)] * len(outs),
        scratch_shapes=list(scratch),
        compiler_params=pltpu.CompilerParams(vmem_limit_bytes=limit),
        cost_estimate=pl.CostEstimate(flops=flops, bytes_accessed=size, transcendentals=0),
    )(*args)


def swap(value, axis, bit):
    count = lax.axis_size(axis)
    return lax.ppermute(value, axis, [(i, i ^ bit) for i in range(count)])


def wave_swap(value, step):
    rows, count = lax.axis_size("atom"), lax.axis_size("wave")
    bits = [count - 1 - step, 1 + step]
    pairs = [(a * count + w, a * count + (w ^ bits[a % CORES])) for a in range(rows) for w in range(count)]
    return lax.ppermute(value, ("atom", "wave"), pairs)


def z_swap(value, step):
    count = lax.axis_size("atom")
    steps = (count // CORES).bit_length() - 1
    bits = [CORES << s for s in range(steps)]
    return lax.ppermute(
        value, "atom", [(i, i ^ bits[step if i % CORES == 0 else steps - 1 - step]) for i in range(count)]
    )


def shards(features, species, coords, wave_index, green, embed, w_charge, w_feat, w_pot, w_out):
    array = jax.ShapeDtypeStruct
    atoms = features.shape[0]
    q = w_charge.shape[1]
    hidden = w_feat.shape[1]
    waves = wave_index.shape[1]
    wcount = lax.axis_size("wave")
    acount = lax.axis_size("atom")
    zcount = acount // CORES
    half_rows = 2 * (waves // CORES)
    rest = (wcount - 1) * atoms

    half = waves // CORES
    pieces = PIECES if (half // min(TILE, half)) % PIECES == 0 else 1
    span = half // pieces
    tile = min(TILE, span)

    hidden_v, mixed, message, waves_v, green_v = call(
        fetch_kernel,
        [
            array(features.shape, BF16), array(features.shape, BF16), array((q + POINT_ROWS, atoms), BF16),
            array(wave_index.shape, jnp.int32), array((1, waves), F32),
        ],
        features, species.reshape(1, atoms), coords, wave_index, green.reshape(1, waves), embed, w_charge.T,
        scratch=[
            pltpu.VMEM((1, atoms), jnp.int32), pltpu.VMEM(coords.shape, F32),
            pltpu.VMEM(embed.shape, BF16), pltpu.VMEM((q, features.shape[1]), BF16),
            pltpu.SemaphoreType.DMA((7,)),
        ],
        space=pltpu.HBM,
    )
    messages = [swap(message, "wave", b) for b in range(1, wcount)]
    n, g, p_own0, p_other0, s_own0, s_other0 = call(
        functools.partial(own_kernel, pieces),
        [
            array((waves, POINT_ROWS), BF16),
            array((1, half_rows), F32),
            array((half_rows, atoms), BF16),
            array((half_rows, atoms), BF16),
            array((q, half_rows), F32),
            array((q, half_rows), F32),
        ],
        waves_v, green_v, message,
        flops=4 * half_rows * atoms * q,
    )

    def rest_call(start, size, s_start, n, s_in, dtype):
        return call(
            functools.partial(rest_kernel, start, size, tile, s_start, wcount - 1),
            [array((2 * size, rest), BF16), array((q, 2 * size), dtype)],
            n, s_in, *messages,
            scratch=[pltpu.VMEM((q, rest), BF16)],
            flops=4 * size * rest * q,
        )

    def join(outs, mine, *got, offset=0):
        return call(
            functools.partial(join_kernel, offset, len(got)), [array(mine.shape, dtype) for dtype in outs], mine, *got
        )

    rows = 2 * span
    p_other, s_other = rest_call(half, half, 0, n, s_other0, BF16)
    got = swap(s_other, "atom", 1)
    p_own, sums, arrived = [], [], []
    for i in range(pieces):
        p, total = rest_call(i * span, span, i * rows, n, s_own0, F32)
        p_own.append(p)
        total, send = join([F32, BF16], total, got, offset=i * rows)
        sums.append(total)
        arrived.append(z_swap(send, 0))
        n, sums[-1] = lax.optimization_barrier((n, sums[-1]))
    for step in range(1, zcount.bit_length() - 1):
        for i in range(pieces):
            sums[i], send = join([F32, BF16], sums[i], arrived[i])
            arrived[i] = z_swap(send, step)
    (w_own,) = call(
        functools.partial(weight_kernel, pieces), [array((q, half_rows), BF16)],
        g, *[value for pair in zip(sums, arrived) for value in pair],
    )
    w_other = swap(w_own, "atom", 1)
    own, others = call(
        functools.partial(potential_kernel, pieces), [array((q, atoms), F32), array((q, rest), F32)],
        w_own, p_own0, *p_own,
        flops=2 * half_rows * (rest + atoms) * q,
    )
    sends = call(
        send_kernel, [array((q, atoms), BF16)] * (wcount - 1), w_other, p_other, others,
        flops=2 * half_rows * rest * q,
    )
    parts = [wave_swap(value, b) for b, value in enumerate(sends)]
    total, pre = call(
        keep_kernel,
        [array((q, atoms), F32), array((atoms, hidden), F32)],
        w_other, p_other0, own, mixed, w_feat,
        flops=2 * half_rows * atoms * q,
    )
    (out,) = call(
        functools.partial(last_kernel, wcount - 1), [array(features.shape, BF16)],
        hidden_v, total, pre, w_pot, w_out, *parts,
        scratch=[pltpu.VMEM(features.shape, BF16), pltpu.SemaphoreType.DMA((OUT_PARTS,))],
        out_space=pl.ANY,
    )
    return out


def solution(mesh):
    placed = (
        P(("atom", "wave"), None),
        P(("atom", "wave")),
        P(None, ("atom", "wave")),
        P(None, "wave"),
        P("wave"),
        P(),
        P(),
        P(),
        P(),
        P(),
    )
    return jax.shard_map(
        shards, mesh=mesh, in_specs=placed, out_specs=P(("atom", "wave"), None), check_vma=False
    )
```

```python
import functools
import math

import jax
import jax.numpy as jnp
import numpy as np
from jax import lax
from jax.experimental import pallas as pl
from jax.experimental.pallas import tpu as pltpu
from jax.sharding import PartitionSpec as P

EPS = 1e-06
F32 = jnp.float32
BF16 = jnp.bfloat16
POINT_ROWS = 16
CORES = 2
TILE = 128
MARGIN = 2e-6
PIECES = 2
OUT_PARTS = 4


def half_sine():
    u = (np.cos(np.pi * np.arange(4) / 3) + 1) / 8
    r = np.sqrt(np.maximum(u, 1e-16))
    return [float(c) for c in np.polynomial.polynomial.polyfit(u, math.sqrt(2) * np.sin(np.pi * r) / r, 3)]


HALF_SINE = half_sine()


def phases(turns):
    r = turns - jnp.round(turns)
    u = r * r
    total = HALF_SINE[-1]
    for c in HALF_SINE[-2::-1]:
        total = total * u + c
    s = total * r
    q = s * s
    rest = (2.0 + MARGIN) - q
    return (1.0 - q).astype(BF16), (s * (rest * lax.rsqrt(rest))).astype(BF16)


def put_phases(p_ref, lo, tile, left, n, x):
    cosine, sine = phases(jnp.dot(n, x, preferred_element_type=F32))
    right = left + x.shape[1]
    p_ref[lo : lo + tile, left:right] = cosine
    p_ref[lo + tile : lo + 2 * tile, left:right] = sine


def nt(a, b):
    return lax.dot_general(a, b, (((1,), (1,)), ((), ())), preferred_element_type=F32)


def tn(a, b):
    return lax.dot_general(a, b, (((0,), (0,)), ((), ())), preferred_element_type=F32)


def triple_rows(values, width):
    row = lax.broadcasted_iota(jnp.int32, (POINT_ROWS, width), 0)
    part = row % 3
    picked = jnp.where(part == 0, values[0:1], jnp.where(part == 1, values[1:2], values[2:3]))
    return row, picked


def fetch_kernel(
    features_ref, species_ref, coords_ref, waves_ref, green_ref, embed_ref, w_charge_ref,
    hidden_ref, mixed_ref, message_ref, waves_out, green_out,
    species_v, coords_v, embed_v, w_charge_v, sems,
):
    pairs = (
        (features_ref, hidden_ref), (embed_ref, embed_v), (species_ref, species_v),
        (w_charge_ref, w_charge_v), (coords_ref, coords_v), (waves_ref, waves_out), (green_ref, green_out),
    )
    copies = [pltpu.make_async_copy(a, b, sems.at[i]) for i, (a, b) in enumerate(pairs)]
    for copy in copies:
        copy.start()
    for copy in copies:
        copy.wait()
    rows = hidden_ref.shape[0]
    q = w_charge_v.shape[0]
    hidden = hidden_ref[...].astype(F32)
    scale = lax.rsqrt(jnp.mean(hidden * hidden, axis=1, keepdims=True) + EPS)
    kinds = embed_v.shape[0]
    onehot = (
        lax.broadcasted_iota(jnp.int32, (kinds, rows), 0) == species_v[...]
    ).astype(F32).astype(BF16)
    mixed = (hidden * scale + tn(onehot, embed_v[...])).astype(BF16)
    mixed_ref[...] = mixed
    message_ref[0:q, :] = nt(w_charge_v[...], mixed).astype(BF16)
    row, point = triple_rows(coords_v[...], rows)
    high = point.astype(BF16).astype(F32)
    middle = (point - high).astype(BF16).astype(F32)
    low = point - high - middle
    parts = jnp.where(row < 3, high, jnp.where(row < 6, middle, jnp.where(row < 9, low, 0.0)))
    message_ref[q:, :] = parts.astype(BF16)


def own_kernel(
    pieces, waves_ref, green_ref, message_ref,
    n_ref, g_ref, p_own_ref, p_other_ref, s_own_ref, s_other_ref,
):
    width = waves_ref.shape[1]
    half = width // CORES
    span = half // pieces
    tile = min(TILE, span)
    q = message_ref.shape[0] - POINT_ROWS
    core = lax.axis_index("atom") % CORES
    row, index = triple_rows(waves_ref[...].astype(F32), width)
    index = jnp.where(row < 9, index, 0.0)

    def pick(values, h, i):
        at = i * span
        first, second = values[:, at : at + span], values[:, half + at : half + at + span]
        return jnp.where(core == h, first, second)

    for h in range(CORES):
        for i in range(pieces):
            at = h * half + i * span
            n_ref[at : at + span, :] = pick(index, h, i).T.astype(BF16)
    for i in range(pieces):
        green = pick(green_ref[...], 0, i)
        for c in range(span // tile):
            g = green[:, c * tile : (c + 1) * tile]
            lo = 2 * (i * span + c * tile)
            g_ref[:, lo : lo + 2 * tile] = jnp.concatenate([g, g], axis=1)
    x = message_ref[q:, :]
    for h, (p_ref, s_ref) in enumerate(((p_own_ref, s_own_ref), (p_other_ref, s_other_ref))):
        for c in range(half // tile):
            lo = 2 * c * tile
            put_phases(p_ref, lo, tile, 0, n_ref[h * half + c * tile : h * half + (c + 1) * tile, :], x)
            s_ref[:, lo : lo + 2 * tile] = nt(message_ref[0:q, :], p_ref[lo : lo + 2 * tile, :])


def rest_kernel(start, span, tile, s_start, count, *refs):
    n_ref, s_in_ref = refs[0], refs[1]
    messages = refs[2 : 2 + count]
    p_ref, s_ref, charges = refs[2 + count :]
    q = messages[0].shape[0] - POINT_ROWS
    atoms = messages[0].shape[1]
    for b, message_ref in enumerate(messages):
        charges[:, b * atoms : (b + 1) * atoms] = message_ref[0:q, :]
    for c in range(span // tile):
        n = n_ref[start + c * tile : start + (c + 1) * tile, :]
        lo, hi = 2 * c * tile, 2 * (c + 1) * tile
        total = s_in_ref[:, s_start + lo : s_start + hi]
        for b, message_ref in enumerate(messages):
            put_phases(p_ref, lo, tile, b * atoms, n, message_ref[q:, :])
            if b == len(messages) - 2:
                total = total + nt(charges[:, : (b + 1) * atoms], p_ref[lo:hi, : (b + 1) * atoms])
        at = (len(messages) - 1) * atoms
        total = total + nt(charges[:, at:], p_ref[lo:hi, at:])
        s_ref[:, lo:hi] = total.astype(s_ref.dtype)


def join_kernel(offset, count, *refs):
    outs = refs[1 + count :]
    width = refs[0].shape[1]
    total = refs[0][...]
    for i, ref in enumerate(refs[1 : 1 + count]):
        at = offset if i == 0 else 0
        total = total + ref[:, at : at + width].astype(F32)
    for ref in outs:
        ref[...] = total.astype(ref.dtype)


def weight_kernel(count, *refs):
    g_ref, out_ref = refs[0], refs[-1]
    at = 0
    for i in range(count):
        mine_ref, got_ref = refs[1 + 2 * i : 3 + 2 * i]
        width = mine_ref.shape[1]
        total = mine_ref[...] + got_ref[...].astype(F32)
        out_ref[:, at : at + width] = (total * g_ref[:, at : at + width]).astype(BF16)
        at += width


def potential_kernel(pieces, w_ref, p0_ref, *refs):
    own_ref, rest_ref = refs[pieces:]
    own_ref[...] = jnp.dot(w_ref[...], p0_ref[...], preferred_element_type=F32)
    at, total = 0, None
    for p_ref in refs[:pieces]:
        height = p_ref.shape[0]
        part = jnp.dot(w_ref[:, at : at + height], p_ref[...], preferred_element_type=F32)
        total = part if total is None else total + part
        at += height
    rest_ref[...] = total


def send_kernel(w_ref, p_ref, rest_ref, *send_refs):
    atoms = send_refs[0].shape[1]
    core = lax.axis_index("atom") % CORES
    for b, ref in enumerate(send_refs):
        block = jnp.where(core == 0, len(send_refs) - 1 - b, b)
        here = pl.ds(pl.multiple_of(block * atoms, atoms), atoms)
        part = jnp.dot(w_ref[...], p_ref[:, here], preferred_element_type=F32)
        ref[...] = (rest_ref[:, here] + part).astype(BF16)


def keep_kernel(w_ref, p0_ref, own_ref, mixed_ref, w_feat_ref, total_ref, pre_ref):
    total_ref[...] = own_ref[...] + jnp.dot(w_ref[...], p0_ref[...], preferred_element_type=F32)
    pre_ref[...] = jnp.dot(mixed_ref[...], w_feat_ref[...], preferred_element_type=F32)


def last_kernel(count, hidden_ref, total_ref, pre_ref, w_pot_ref, w_out_ref, *refs):
    out_ref, out_v, sems = refs[count:]
    atoms = hidden_ref.shape[0]
    step = atoms // OUT_PARTS
    copies = []
    for i in range(OUT_PARTS):
        at = i * step
        potential = total_ref[:, at : at + step]
        for ref in refs[:count]:
            potential = potential + ref[:, at : at + step].astype(F32)
        pre = pre_ref[at : at + step, :] + tn(potential.astype(BF16), w_pot_ref[...])
        activation = (0.5 * pre * (1.0 + jnp.tanh(0.5 * pre))).astype(BF16)
        out = hidden_ref[at : at + step, :].astype(F32) + jnp.dot(
            activation, w_out_ref[...], preferred_element_type=F32
        )
        out_v[at : at + step, :] = out.astype(BF16)
        copy = pltpu.make_async_copy(out_v.at[at : at + step, :], out_ref.at[at : at + step, :], sems.at[i])
        copy.start()
        copies.append(copy)
    for copy in copies:
        copy.wait()


def call(kernel, outs, *args, scratch=(), flops=0, space=pltpu.VMEM, out_space=pltpu.VMEM):
    size = sum(math.prod(a.shape) * a.dtype.itemsize for a in (*args, *outs))
    limit = min(max(4 * size, 16 << 20), 56 << 20)
    if space == pltpu.HBM:
        args = [pltpu.with_memory_space_constraint(a, pltpu.HBM) for a in args]
    return pl.pallas_call(
        kernel,
        out_shape=outs,
        in_specs=[pl.BlockSpec(memory_space=space)] * len(args),
        out_specs=[pl.BlockSpec(memory_space=out_space)] * len(outs),
        scratch_shapes=list(scratch),
        compiler_params=pltpu.CompilerParams(vmem_limit_bytes=limit),
        cost_estimate=pl.CostEstimate(flops=flops, bytes_accessed=size, transcendentals=0),
    )(*args)


def swap(value, axis, bit):
    count = lax.axis_size(axis)
    return lax.ppermute(value, axis, [(i, i ^ bit) for i in range(count)])


def wave_swap(value, step):
    rows, count = lax.axis_size("atom"), lax.axis_size("wave")
    bits = [count - 1 - step, 1 + step]
    pairs = [(a * count + w, a * count + (w ^ bits[a % CORES])) for a in range(rows) for w in range(count)]
    return lax.ppermute(value, ("atom", "wave"), pairs)


def z_swap(value, step):
    count = lax.axis_size("atom")
    steps = (count // CORES).bit_length() - 1
    bits = [CORES << s for s in range(steps)]
    return lax.ppermute(
        value, "atom", [(i, i ^ bits[step if i % CORES == 0 else steps - 1 - step]) for i in range(count)]
    )


def shards(features, species, coords, wave_index, green, embed, w_charge, w_feat, w_pot, w_out):
    array = jax.ShapeDtypeStruct
    atoms = features.shape[0]
    q = w_charge.shape[1]
    hidden = w_feat.shape[1]
    waves = wave_index.shape[1]
    wcount = lax.axis_size("wave")
    acount = lax.axis_size("atom")
    zcount = acount // CORES
    half_rows = 2 * (waves // CORES)
    rest = (wcount - 1) * atoms

    half = waves // CORES
    pieces = PIECES if (half // min(TILE, half)) % PIECES == 0 else 1
    span = half // pieces
    tile = min(TILE, span)

    hidden_v, mixed, message, waves_v, green_v = call(
        fetch_kernel,
        [
            array(features.shape, BF16), array(features.shape, BF16), array((q + POINT_ROWS, atoms), BF16),
            array(wave_index.shape, jnp.int32), array((1, waves), F32),
        ],
        features, species.reshape(1, atoms), coords, wave_index, green.reshape(1, waves), embed, w_charge.T,
        scratch=[
            pltpu.VMEM((1, atoms), jnp.int32), pltpu.VMEM(coords.shape, F32),
            pltpu.VMEM(embed.shape, BF16), pltpu.VMEM((q, features.shape[1]), BF16),
            pltpu.SemaphoreType.DMA((7,)),
        ],
        space=pltpu.HBM,
    )
    messages = [swap(message, "wave", b) for b in range(1, wcount)]
    n, g, p_own0, p_other0, s_own0, s_other0 = call(
        functools.partial(own_kernel, pieces),
        [
            array((waves, POINT_ROWS), BF16),
            array((1, half_rows), F32),
            array((half_rows, atoms), BF16),
            array((half_rows, atoms), BF16),
            array((q, half_rows), F32),
            array((q, half_rows), F32),
        ],
        waves_v, green_v, message,
        flops=4 * half_rows * atoms * q,
    )

    def rest_call(start, size, s_start, n, s_in, dtype):
        return call(
            functools.partial(rest_kernel, start, size, tile, s_start, wcount - 1),
            [array((2 * size, rest), BF16), array((q, 2 * size), dtype)],
            n, s_in, *messages,
            scratch=[pltpu.VMEM((q, rest), BF16)],
            flops=4 * size * rest * q,
        )

    def join(outs, mine, *got, offset=0):
        return call(
            functools.partial(join_kernel, offset, len(got)), [array(mine.shape, dtype) for dtype in outs], mine, *got
        )

    rows = 2 * span
    p_other, s_other = rest_call(half, half, 0, n, s_other0, BF16)
    got = swap(s_other, "atom", 1)
    p_own, sums, arrived = [], [], []
    for i in range(pieces):
        p, total = rest_call(i * span, span, i * rows, n, s_own0, F32)
        p_own.append(p)
        total, send = join([F32, BF16], total, got, offset=i * rows)
        sums.append(total)
        arrived.append(z_swap(send, 0))
        n, sums[-1] = lax.optimization_barrier((n, sums[-1]))
    for step in range(1, zcount.bit_length() - 1):
        for i in range(pieces):
            sums[i], send = join([F32, BF16], sums[i], arrived[i])
            arrived[i] = z_swap(send, step)
    (w_own,) = call(
        functools.partial(weight_kernel, pieces), [array((q, half_rows), BF16)],
        g, *[value for pair in zip(sums, arrived) for value in pair],
    )
    w_other = swap(w_own, "atom", 1)
    own, others = call(
        functools.partial(potential_kernel, pieces), [array((q, atoms), F32), array((q, rest), F32)],
        w_own, p_own0, *p_own,
        flops=2 * half_rows * (rest + atoms) * q,
    )
    sends = call(
        send_kernel, [array((q, atoms), BF16)] * (wcount - 1), w_other, p_other, others,
        flops=2 * half_rows * rest * q,
    )
    parts = [wave_swap(value, b) for b, value in enumerate(sends)]
    total, pre = call(
        keep_kernel,
        [array((q, atoms), F32), array((atoms, hidden), F32)],
        w_other, p_other0, own, mixed, w_feat,
        flops=2 * half_rows * atoms * q,
    )
    (out,) = call(
        functools.partial(last_kernel, wcount - 1), [array(features.shape, BF16)],
        hidden_v, total, pre, w_pot, w_out, *parts,
        scratch=[pltpu.VMEM(features.shape, BF16), pltpu.SemaphoreType.DMA((OUT_PARTS,))],
        out_space=pl.ANY,
    )
    return out


def solution(mesh):
    placed = (
        P(("atom", "wave"), None),
        P(("atom", "wave")),
        P(None, ("atom", "wave")),
        P(None, "wave"),
        P("wave"),
        P(),
        P(),
        P(),
        P(),
        P(),
    )
    return jax.shard_map(
        shards, mesh=mesh, in_specs=placed, out_specs=P(("atom", "wave"), None), check_vma=False
    )
```

```python
import functools
import math

import jax
import jax.numpy as jnp
import numpy as np
from jax import lax
from jax.experimental import pallas as pl
from jax.experimental.pallas import tpu as pltpu
from jax.sharding import PartitionSpec as P

EPS = 1e-06
F32 = jnp.float32
BF16 = jnp.bfloat16
POINT_ROWS = 16
CORES = 2
TILE = 128
MARGIN = 2e-6
PIECES = 2
OUT_PARTS = 4


def half_sine():
    u = (np.cos(np.pi * np.arange(4) / 3) + 1) / 8
    r = np.sqrt(np.maximum(u, 1e-16))
    return [float(c) for c in np.polynomial.polynomial.polyfit(u, math.sqrt(2) * np.sin(np.pi * r) / r, 3)]


HALF_SINE = half_sine()


def phases(turns):
    r = turns - jnp.round(turns)
    u = r * r
    total = HALF_SINE[-1]
    for c in HALF_SINE[-2::-1]:
        total = total * u + c
    s = total * r
    q = s * s
    rest = (2.0 + MARGIN) - q
    return (1.0 - q).astype(BF16), (s * (rest * lax.rsqrt(rest))).astype(BF16)


def put_phases(p_ref, lo, tile, left, n, x):
    cosine, sine = phases(jnp.dot(n, x, preferred_element_type=F32))
    right = left + x.shape[1]
    p_ref[lo : lo + tile, left:right] = cosine
    p_ref[lo + tile : lo + 2 * tile, left:right] = sine


def nt(a, b):
    return lax.dot_general(a, b, (((1,), (1,)), ((), ())), preferred_element_type=F32)


def tn(a, b):
    return lax.dot_general(a, b, (((0,), (0,)), ((), ())), preferred_element_type=F32)


def triple_rows(values, width):
    row = lax.broadcasted_iota(jnp.int32, (POINT_ROWS, width), 0)
    part = row % 3
    picked = jnp.where(part == 0, values[0:1], jnp.where(part == 1, values[1:2], values[2:3]))
    return row, picked


def fetch_kernel(
    features_ref, species_ref, coords_ref, waves_ref, green_ref, embed_ref, w_charge_ref,
    hidden_ref, mixed_ref, message_ref, waves_out, green_out,
    species_v, coords_v, embed_v, w_charge_v, sems,
):
    pairs = (
        (features_ref, hidden_ref), (embed_ref, embed_v), (species_ref, species_v),
        (w_charge_ref, w_charge_v), (coords_ref, coords_v), (waves_ref, waves_out), (green_ref, green_out),
    )
    copies = [pltpu.make_async_copy(a, b, sems.at[i]) for i, (a, b) in enumerate(pairs)]
    for copy in copies:
        copy.start()
    for copy in copies:
        copy.wait()
    rows = hidden_ref.shape[0]
    q = w_charge_v.shape[0]
    hidden = hidden_ref[...].astype(F32)
    scale = lax.rsqrt(jnp.mean(hidden * hidden, axis=1, keepdims=True) + EPS)
    kinds = embed_v.shape[0]
    onehot = (
        lax.broadcasted_iota(jnp.int32, (kinds, rows), 0) == species_v[...]
    ).astype(F32).astype(BF16)
    mixed = (hidden * scale + tn(onehot, embed_v[...])).astype(BF16)
    mixed_ref[...] = mixed
    message_ref[0:q, :] = nt(w_charge_v[...], mixed).astype(BF16)
    row, point = triple_rows(coords_v[...], rows)
    high = point.astype(BF16).astype(F32)
    middle = (point - high).astype(BF16).astype(F32)
    low = point - high - middle
    parts = jnp.where(row < 3, high, jnp.where(row < 6, middle, jnp.where(row < 9, low, 0.0)))
    message_ref[q:, :] = parts.astype(BF16)


def own_kernel(
    pieces, waves_ref, green_ref, message_ref,
    n_ref, g_ref, p_own_ref, p_other_ref, s_own_ref, s_other_ref,
):
    width = waves_ref.shape[1]
    half = width // CORES
    span = half // pieces
    tile = min(TILE, span)
    q = message_ref.shape[0] - POINT_ROWS
    core = lax.axis_index("atom") % CORES
    row, index = triple_rows(waves_ref[...].astype(F32), width)
    index = jnp.where(row < 9, index, 0.0)

    def pick(values, h, i):
        at = i * span
        first, second = values[:, at : at + span], values[:, half + at : half + at + span]
        return jnp.where(core == h, first, second)

    for h in range(CORES):
        for i in range(pieces):
            at = h * half + i * span
            n_ref[at : at + span, :] = pick(index, h, i).T.astype(BF16)
    for i in range(pieces):
        green = pick(green_ref[...], 0, i)
        for c in range(span // tile):
            g = green[:, c * tile : (c + 1) * tile]
            lo = 2 * (i * span + c * tile)
            g_ref[:, lo : lo + 2 * tile] = jnp.concatenate([g, g], axis=1)
    x = message_ref[q:, :]
    for h, (p_ref, s_ref) in enumerate(((p_own_ref, s_own_ref), (p_other_ref, s_other_ref))):
        for c in range(half // tile):
            lo = 2 * c * tile
            put_phases(p_ref, lo, tile, 0, n_ref[h * half + c * tile : h * half + (c + 1) * tile, :], x)
            s_ref[:, lo : lo + 2 * tile] = nt(message_ref[0:q, :], p_ref[lo : lo + 2 * tile, :])


def rest_kernel(start, span, tile, s_start, count, *refs):
    n_ref, s_in_ref = refs[0], refs[1]
    messages = refs[2 : 2 + count]
    p_ref, s_ref, charges = refs[2 + count :]
    q = messages[0].shape[0] - POINT_ROWS
    atoms = messages[0].shape[1]
    for b, message_ref in enumerate(messages):
        charges[:, b * atoms : (b + 1) * atoms] = message_ref[0:q, :]
    for c in range(span // tile):
        n = n_ref[start + c * tile : start + (c + 1) * tile, :]
        lo, hi = 2 * c * tile, 2 * (c + 1) * tile
        total = s_in_ref[:, s_start + lo : s_start + hi]
        for b, message_ref in enumerate(messages):
            put_phases(p_ref, lo, tile, b * atoms, n, message_ref[q:, :])
            if b == len(messages) - 2:
                total = total + nt(charges[:, : (b + 1) * atoms], p_ref[lo:hi, : (b + 1) * atoms])
        at = (len(messages) - 1) * atoms
        total = total + nt(charges[:, at:], p_ref[lo:hi, at:])
        s_ref[:, lo:hi] = total.astype(s_ref.dtype)


def join_kernel(offset, count, *refs):
    outs = refs[1 + count :]
    width = refs[0].shape[1]
    total = refs[0][...]
    for i, ref in enumerate(refs[1 : 1 + count]):
        at = offset if i == 0 else 0
        total = total + ref[:, at : at + width].astype(F32)
    for ref in outs:
        ref[...] = total.astype(ref.dtype)


def weight_kernel(count, *refs):
    g_ref, out_ref = refs[0], refs[-1]
    at = 0
    for i in range(count):
        mine_ref, got_ref = refs[1 + 2 * i : 3 + 2 * i]
        width = mine_ref.shape[1]
        total = mine_ref[...] + got_ref[...].astype(F32)
        out_ref[:, at : at + width] = (total * g_ref[:, at : at + width]).astype(BF16)
        at += width


def potential_kernel(pieces, w_ref, p0_ref, *refs):
    own_ref, rest_ref = refs[pieces:]
    own_ref[...] = jnp.dot(w_ref[...], p0_ref[...], preferred_element_type=F32)
    at, total = 0, None
    for p_ref in refs[:pieces]:
        height = p_ref.shape[0]
        part = jnp.dot(w_ref[:, at : at + height], p_ref[...], preferred_element_type=F32)
        total = part if total is None else total + part
        at += height
    rest_ref[...] = total


def send_kernel(w_ref, p_ref, rest_ref, *send_refs):
    atoms = send_refs[0].shape[1]
    core = lax.axis_index("atom") % CORES
    for b, ref in enumerate(send_refs):
        block = jnp.where(core == 0, len(send_refs) - 1 - b, b)
        here = pl.ds(pl.multiple_of(block * atoms, atoms), atoms)
        part = jnp.dot(w_ref[...], p_ref[:, here], preferred_element_type=F32)
        ref[...] = (rest_ref[:, here] + part).astype(BF16)


def keep_kernel(w_ref, p0_ref, own_ref, mixed_ref, w_feat_ref, total_ref, pre_ref):
    total_ref[...] = own_ref[...] + jnp.dot(w_ref[...], p0_ref[...], preferred_element_type=F32)
    pre_ref[...] = jnp.dot(mixed_ref[...], w_feat_ref[...], preferred_element_type=F32)


def last_kernel(count, hidden_ref, total_ref, pre_ref, w_pot_ref, w_out_ref, *refs):
    out_ref, out_v, sems = refs[count:]
    atoms = hidden_ref.shape[0]
    step = atoms // OUT_PARTS
    copies = []
    for i in range(OUT_PARTS):
        at = i * step
        potential = total_ref[:, at : at + step]
        for ref in refs[:count]:
            potential = potential + ref[:, at : at + step].astype(F32)
        pre = pre_ref[at : at + step, :] + tn(potential.astype(BF16), w_pot_ref[...])
        activation = (0.5 * pre * (1.0 + jnp.tanh(0.5 * pre))).astype(BF16)
        out = hidden_ref[at : at + step, :].astype(F32) + jnp.dot(
            activation, w_out_ref[...], preferred_element_type=F32
        )
        out_v[at : at + step, :] = out.astype(BF16)
        copy = pltpu.make_async_copy(out_v.at[at : at + step, :], out_ref.at[at : at + step, :], sems.at[i])
        copy.start()
        copies.append(copy)
    for copy in copies:
        copy.wait()


def call(kernel, outs, *args, scratch=(), flops=0, space=pltpu.VMEM, out_space=pltpu.VMEM):
    size = sum(math.prod(a.shape) * a.dtype.itemsize for a in (*args, *outs))
    limit = min(max(4 * size, 16 << 20), 56 << 20)
    if space == pltpu.HBM:
        args = [pltpu.with_memory_space_constraint(a, pltpu.HBM) for a in args]
    return pl.pallas_call(
        kernel,
        out_shape=outs,
        in_specs=[pl.BlockSpec(memory_space=space)] * len(args),
        out_specs=[pl.BlockSpec(memory_space=out_space)] * len(outs),
        scratch_shapes=list(scratch),
        compiler_params=pltpu.CompilerParams(vmem_limit_bytes=limit),
        cost_estimate=pl.CostEstimate(flops=flops, bytes_accessed=size, transcendentals=0),
    )(*args)


def swap(value, axis, bit):
    count = lax.axis_size(axis)
    return lax.ppermute(value, axis, [(i, i ^ bit) for i in range(count)])


def wave_swap(value, step):
    rows, count = lax.axis_size("atom"), lax.axis_size("wave")
    bits = [count - 1 - step, 1 + step]
    pairs = [(a * count + w, a * count + (w ^ bits[a % CORES])) for a in range(rows) for w in range(count)]
    return lax.ppermute(value, ("atom", "wave"), pairs)


def z_swap(value, step):
    count = lax.axis_size("atom")
    steps = (count // CORES).bit_length() - 1
    bits = [CORES << s for s in range(steps)]
    return lax.ppermute(
        value, "atom", [(i, i ^ bits[step if i % CORES == 0 else steps - 1 - step]) for i in range(count)]
    )


def shards(features, species, coords, wave_index, green, embed, w_charge, w_feat, w_pot, w_out):
    array = jax.ShapeDtypeStruct
    atoms = features.shape[0]
    q = w_charge.shape[1]
    hidden = w_feat.shape[1]
    waves = wave_index.shape[1]
    wcount = lax.axis_size("wave")
    acount = lax.axis_size("atom")
    zcount = acount // CORES
    half_rows = 2 * (waves // CORES)
    rest = (wcount - 1) * atoms

    half = waves // CORES
    pieces = PIECES if (half // min(TILE, half)) % PIECES == 0 else 1
    span = half // pieces
    tile = min(TILE, span)

    hidden_v, mixed, message, waves_v, green_v = call(
        fetch_kernel,
        [
            array(features.shape, BF16), array(features.shape, BF16), array((q + POINT_ROWS, atoms), BF16),
            array(wave_index.shape, jnp.int32), array((1, waves), F32),
        ],
        features, species.reshape(1, atoms), coords, wave_index, green.reshape(1, waves), embed, w_charge.T,
        scratch=[
            pltpu.VMEM((1, atoms), jnp.int32), pltpu.VMEM(coords.shape, F32),
            pltpu.VMEM(embed.shape, BF16), pltpu.VMEM((q, features.shape[1]), BF16),
            pltpu.SemaphoreType.DMA((7,)),
        ],
        space=pltpu.HBM,
    )
    messages = [swap(message, "wave", b) for b in range(1, wcount)]
    n, g, p_own0, p_other0, s_own0, s_other0 = call(
        functools.partial(own_kernel, pieces),
        [
            array((waves, POINT_ROWS), BF16),
            array((1, half_rows), F32),
            array((half_rows, atoms), BF16),
            array((half_rows, atoms), BF16),
            array((q, half_rows), F32),
            array((q, half_rows), F32),
        ],
        waves_v, green_v, message,
        flops=4 * half_rows * atoms * q,
    )

    def rest_call(start, size, s_start, n, s_in, dtype):
        return call(
            functools.partial(rest_kernel, start, size, tile, s_start, wcount - 1),
            [array((2 * size, rest), BF16), array((q, 2 * size), dtype)],
            n, s_in, *messages,
            scratch=[pltpu.VMEM((q, rest), BF16)],
            flops=4 * size * rest * q,
        )

    def join(outs, mine, *got, offset=0):
        return call(
            functools.partial(join_kernel, offset, len(got)), [array(mine.shape, dtype) for dtype in outs], mine, *got
        )

    rows = 2 * span
    p_other, s_other = rest_call(half, half, 0, n, s_other0, BF16)
    got = swap(s_other, "atom", 1)
    p_own, sums, arrived = [], [], []
    for i in range(pieces):
        p, total = rest_call(i * span, span, i * rows, n, s_own0, F32)
        p_own.append(p)
        total, send = join([F32, BF16], total, got, offset=i * rows)
        sums.append(total)
        arrived.append(z_swap(send, 0))
    for step in range(1, zcount.bit_length() - 1):
        for i in range(pieces):
            sums[i], send = join([F32, BF16], sums[i], arrived[i])
            arrived[i] = z_swap(send, step)
    (w_own,) = call(
        functools.partial(weight_kernel, pieces), [array((q, half_rows), BF16)],
        g, *[value for pair in zip(sums, arrived) for value in pair],
    )
    w_other = swap(w_own, "atom", 1)
    own, others = call(
        functools.partial(potential_kernel, pieces), [array((q, atoms), F32), array((q, rest), F32)],
        w_own, p_own0, *p_own,
        flops=2 * half_rows * (rest + atoms) * q,
    )
    sends = call(
        send_kernel, [array((q, atoms), BF16)] * (wcount - 1), w_other, p_other, others,
        flops=2 * half_rows * rest * q,
    )
    parts = [wave_swap(value, b) for b, value in enumerate(sends)]
    total, pre = call(
        keep_kernel,
        [array((q, atoms), F32), array((atoms, hidden), F32)],
        w_other, p_other0, own, mixed, w_feat,
        flops=2 * half_rows * atoms * q,
    )
    (out,) = call(
        functools.partial(last_kernel, wcount - 1), [array(features.shape, BF16)],
        hidden_v, total, pre, w_pot, w_out, *parts,
        scratch=[pltpu.VMEM(features.shape, BF16), pltpu.SemaphoreType.DMA((OUT_PARTS,))],
        out_space=pl.ANY,
    )
    return out


def solution(mesh):
    placed = (
        P(("atom", "wave"), None),
        P(("atom", "wave")),
        P(None, ("atom", "wave")),
        P(None, "wave"),
        P("wave"),
        P(),
        P(),
        P(),
        P(),
        P(),
    )
    return jax.shard_map(
        shards, mesh=mesh, in_specs=placed, out_specs=P(("atom", "wave"), None), check_vma=False
    )
```
